32 devices in a mesh: dp: 16 (over z, y, x), tensor: 2 (over core).
Axes of the slice: x: 2, y: 2, z: 4, core: 2. Of those that a mesh axis runs over, the one named last changes fastest.
Arguments:
- tokens: bfloat16 [1024, 16, 768], P('tensor', 'dp'), may hold values from -6 to 6
- cotangent: bfloat16 [1024, 16, 768], P('tensor', 'dp'), may hold values from -6 to 6
- segments: int32 [1024, 16], P(None, 'dp'), may hold values from 0 to 6, as said below
- routes: int32 [1024, 16], P('tensor', 'dp'), may hold values from 0 to 15, as said below
- capacity_slot: int32 [1024, 16], P('tensor', 'dp'), may hold values from -1 to 39, as said below
- bucket_index: int32 [2047], replicated, may hold values from 0 to 31
- first_gain: bfloat16 [768], replicated, may hold values from 0.5 to 1.5
- query_projection_matrix: bfloat16 [768, 768], P(None, 'tensor'), may hold values from -0.21875 to 0.21875
- key_projection_matrix: bfloat16 [768, 768], P(None, 'tensor'), may hold values from -0.21875 to 0.21875
- value_projection_matrix: bfloat16 [768, 768], P(None, 'tensor'), may hold values from -0.21875 to 0.21875
- output_projection_matrix: bfloat16 [768, 768], P('tensor'), may hold values from -1.25 to 1.25
- position_bias: bfloat16 [32, 12], P(None, 'tensor'), may hold values from -4 to 4
- second_gain: bfloat16 [768], replicated, may hold values from 0.5 to 1.5
- router_weight: bfloat16 [768, 16], replicated, may hold values from -0.21875 to 0.21875
- expert_in: bfloat16 [16, 768, 3072], P('dp', None, 'tensor'), may hold values from -0.21875 to 0.21875
- expert_out: bfloat16 [16, 3072, 768], P('dp', 'tensor'), may hold values from -6 to 6
Outputs:
- layer_out: bfloat16 [1024, 16, 768], P('tensor', 'dp')
- tokens_grad: bfloat16 [1024, 16, 768], P('tensor', 'dp')
- first_gain_grad: float32 [768], replicated
- query_grad: float32 [768, 768], P(None, 'tensor')
- key_grad: float32 [768, 768], P(None, 'tensor')
- value_grad: float32 [768, 768], P(None, 'tensor')
- output_grad: float32 [768, 768], P('tensor')
- position_bias_grad: float32 [32, 12], P(None, 'tensor')
- second_gain_grad: float32 [768], replicated
- router_grad: float32 [768, 16], replicated
- expert_in_grad: float32 [16, 768, 3072], P('dp', None, 'tensor')
- expert_out_grad: float32 [16, 3072, 768], P('dp', 'tensor')
The draws below stay inside these ranges and needn't reach their ends.
Inputs may be any that keep to these rules, and one draw needn't show every extreme that they name: `routes`: each token's expert. Among the tokens of one device, one expert is chosen by 40 tokens or more, on every device. `capacity_slot`: A token's row in its expert's buffer on its device, or -1 for a dropped token. The tokens of one device with the same expert take rows 0, 1, 2 and so on in order of position and then of sequence; those beyond 40 are dropped. On every device one expert fills all 40 rows. `segments`: never falls along the positions of a sequence; every sequence holds exactly 7 documents, numbered 0 to 6.
All inputs are finite; a program needn't handle non-finite values.
Results may differ from the reference program's by a relative error of at most 0.019.
Values may be sent and summed in bfloat16 or wider, within the bound.
A program may use at most 256 MiB of HBM per device.

```python
import jax
import jax.numpy as jnp
from jax import lax

D = 768
HEADS = 12
HEAD_DIM = 64
FF = 3072
BUCKETS = 32
SEQ_LEN = 1024
SEQ_DEV = 1
INNER = 768
EXPERTS = 16
SEQS = 16
CAP = 40
N_DP = 16
N_TENSOR = 2


def block_routes(key):
    block_total = N_TENSOR * N_DP
    block_size = SEQ_DEV * SEQ_LEN // N_TENSOR
    popular = max(EXPERTS // 4, 1)
    order = jax.random.permutation(jax.random.fold_in(key, 11), EXPERTS)
    even = jax.random.randint(jax.random.fold_in(key, 12), (block_total, block_size), 0, EXPERTS)
    favoured = order[jax.random.randint(jax.random.fold_in(key, 13), (block_total, block_size), 0, popular)]
    picker = jax.random.randint(jax.random.fold_in(key, 14), (block_total, block_size), 0, 4)
    chosen = jnp.where(picker == 0, favoured, even)
    block_keys = jax.random.split(jax.random.fold_in(key, 15), block_total)
    forced = jax.vmap(lambda sub_key: jax.random.permutation(sub_key, block_size))(block_keys)
    chosen = jnp.where(forced < CAP, order[0], chosen).astype(jnp.int32)

    def place(row_routes):
        table = (row_routes[:, None] == jnp.arange(EXPERTS, dtype=jnp.int32)[None, :]).astype(jnp.int32)
        ranks = jnp.sum(jnp.cumsum(table, axis=0) * table, axis=1) - 1
        return jnp.where(ranks < CAP, ranks, -1).astype(jnp.int32)
    places = lax.map(place, chosen)
    return (chosen, places)


def to_grid(blocks):
    block_len = SEQ_LEN // N_TENSOR
    shaped = blocks.reshape(N_TENSOR, N_DP, block_len, SEQ_DEV)
    return jnp.transpose(shaped, (0, 2, 1, 3)).reshape(SEQ_LEN, SEQS).astype(jnp.int32)


def draw_routes(key, part):
    chosen, places = block_routes(key)
    return to_grid(chosen)


def draw_capacity_slot(key, part):
    chosen, places = block_routes(key)
    return to_grid(places)


def draw_segments(key, part):
    key = jax.random.fold_in(key, 3)
    position = jnp.arange(SEQ_LEN, dtype=jnp.int32)[:, None]
    quiet = (position >= 3 * SEQ_LEN // 8) & (position < 5 * SEQ_LEN // 8) | (position == 0)
    scores = jax.random.randint(key, (SEQ_LEN, SEQS), 0, SEQ_LEN)
    distinct = jnp.where(quiet, -1, scores * SEQ_LEN + position)
    top_values, top_places = lax.top_k(distinct.T, 6)
    picked = jnp.arange(SEQ_LEN, dtype=jnp.int32)[None, None, :] == top_places[:, :, None]
    marks = jnp.sum(picked.astype(jnp.int32), axis=1).T
    return jnp.cumsum(marks, axis=0).astype(jnp.int32)


def touch_ends(drawn, own_key, least, high):
    longest = drawn.shape.index(max(drawn.shape))
    spots = []
    for shift in (0, 1):
        where = [jax.random.randint(jax.random.fold_in(own_key, axis), (), 0, length) for axis, length in enumerate(drawn.shape)]
        where[longest] = (where[longest] + shift) % drawn.shape[longest]
        spots.append(tuple(where))
    return drawn.at[spots[0]].set(least).at[spots[1]].set(high)


def block_levels(stream_key, dims, cuts, smallest, high):
    gain, own = 1.0, jax.random.fold_in(stream_key, 6)
    for dim, parts in cuts:
        heights = jnp.exp(jax.random.uniform(jax.random.fold_in(own, dim), (parts,), jnp.float32, smallest / len(cuts), high / len(cuts)))
        gain = gain * jnp.repeat(heights, dims[dim] // parts).reshape([-1 if axis == dim else 1 for axis in range(len(dims))])
    return gain


def centred(stream_key, extent, deviation, bound, cuts=(), kind=jnp.bfloat16):
    array = deviation * jax.random.normal(stream_key, extent, jnp.float32)
    if cuts:
        array = array * block_levels(stream_key, extent, cuts, -0.22, 0.18)
    return jnp.clip(array, -bound, bound).astype(kind)


def setup_inputs(seed: int = 0) -> dict:
    streams_of = jax.random.split(jax.random.key(seed), 17)
    tokens = centred(streams_of[0], (SEQ_LEN, SEQS, D), 1.0, 6.0, ((0, 2), (1, 16)))
    cotangent = centred(streams_of[1], (SEQ_LEN, SEQS, D), 1.0, 6.0, ((0, 2), (1, 16)))
    segments = draw_segments(jax.random.fold_in(streams_of[16], 71), 0)
    routes = draw_routes(jax.random.fold_in(streams_of[16], 71), 0)
    capacity_slot = draw_capacity_slot(jax.random.fold_in(streams_of[16], 71), 0)
    bucket_index = touch_ends(jax.random.randint(streams_of[5], (2 * SEQ_LEN - 1,), 0, BUCKETS), jax.random.fold_in(streams_of[5], 1), 0, BUCKETS - 1).astype(jnp.int32)
    first_gain = jnp.clip(1.0 + 0.1 * jax.random.normal(streams_of[6], (D,), jnp.float32), 0.5, 1.5).astype(jnp.bfloat16)
    query_projection_matrix = centred(streams_of[7], (D, INNER), D ** -0.5, 0.21875, ((1, 2),))
    key_projection_matrix = centred(streams_of[8], (D, INNER), D ** -0.5, 0.21875, ((1, 2),))
    value_projection_matrix = centred(streams_of[9], (D, INNER), D ** -0.5, 0.21875, ((1, 2),))
    output_projection_matrix = centred(streams_of[10], (INNER, D), (INNER // 32) ** -0.5, 1.25, ((0, 2),))
    position_bias = centred(streams_of[11], (BUCKETS, HEADS), 1.0, 4.0, ((1, 2),))
    second_gain = jnp.clip(1.0 + 0.1 * jax.random.normal(streams_of[12], (D,), jnp.float32), 0.5, 1.5).astype(jnp.bfloat16)
    router_weight = centred(streams_of[13], (D, EXPERTS), D ** -0.5, 0.21875)
    expert_in = centred(streams_of[14], (EXPERTS, D, FF), D ** -0.5, 0.21875, ((0, 16), (2, 2)))
    expert_out = centred(streams_of[15], (EXPERTS, FF, D), (1.5 * EXPERTS / FF ** 0.5), 6.0, ((0, 16), (1, 2)))
    return dict(tokens=tokens, cotangent=cotangent, segments=segments, routes=routes, capacity_slot=capacity_slot, bucket_index=bucket_index, first_gain=first_gain, query_projection_matrix=query_projection_matrix, key_projection_matrix=key_projection_matrix, value_projection_matrix=value_projection_matrix, output_projection_matrix=output_projection_matrix, position_bias=position_bias, second_gain=second_gain, router_weight=router_weight, expert_in=expert_in, expert_out=expert_out)


@jax.custom_vjp
def reduced_precision(v):
    return lax.optimization_barrier(v.astype(jnp.bfloat16)).astype(jnp.float32)

@jax.custom_vjp
def reduced_precision_reverse(v):
    return v

def low_keep(v):
    return (reduced_precision(v), None)

def low_pass(kept, grad):
    return (grad,)

def back_keep(v):
    return (v, None)

def back_low(kept, grad):
    return (reduced_precision(grad),)
reduced_precision.defvjp(low_keep, low_pass)
reduced_precision_reverse.defvjp(back_keep, back_low)
epsilon = 1e-06
exact_precision = lax.Precision.HIGHEST

def rms_scale(values):
    return lax.rsqrt(lax.optimization_barrier(jnp.mean(values * values, axis=-1, keepdims=True)) + epsilon)

def expert_apply(pieces):
    buffer_rows, first_matrix, second_matrix = pieces
    pre_act = reduced_precision_reverse(jnp.dot(buffer_rows, first_matrix, precision=exact_precision))
    hidden = reduced_precision(jax.nn.gelu(pre_act, approximate=True))
    return reduced_precision(reduced_precision_reverse(jnp.dot(hidden, second_matrix, precision=exact_precision)))

def layer(segments, routes, capacity_slot, bucket_index, tokens, first_gain, query_projection_matrix, key_projection_matrix, value_projection_matrix, output_projection_matrix, position_bias, second_gain, router_weight, expert_in, expert_out):
    normalized_rows = reduced_precision(tokens * rms_scale(tokens) * first_gain)
    projected_queries = reduced_precision(reduced_precision_reverse(jnp.einsum('cjt,tm->cjm', normalized_rows, query_projection_matrix, precision=exact_precision)))
    projected_keys = reduced_precision(reduced_precision_reverse(jnp.einsum('cjt,tm->cjm', normalized_rows, key_projection_matrix, precision=exact_precision)))
    projected_values = reduced_precision(reduced_precision_reverse(jnp.einsum('cjt,tm->cjm', normalized_rows, value_projection_matrix, precision=exact_precision)))
    offsets = jnp.arange(SEQ_LEN, dtype=jnp.int32)[None, :] - jnp.arange(SEQ_LEN, dtype=jnp.int32)[:, None] + SEQ_LEN - 1
    bias_grid = jnp.transpose(position_bias[bucket_index][offsets], (2, 0, 1))
    score_scale = HEAD_DIM ** (-0.5)

    def attend(pieces):
        query_seq, key_seq, value_seq, segment_seq = pieces
        raw_scores = jnp.einsum('qhd,khd->hqk', query_seq, key_seq, precision=exact_precision) * score_scale + bias_grid
        raw_scores = reduced_precision_reverse(raw_scores)
        same_doc = segment_seq[:, None] == segment_seq[None, :]
        masked = jnp.where(same_doc[None], raw_scores, -1e+30)
        largest = lax.optimization_barrier(jnp.max(masked, axis=-1, keepdims=True))
        weights = jnp.exp(masked - largest)
        probability = reduced_precision(weights / lax.optimization_barrier(jnp.sum(weights, axis=-1, keepdims=True)))
        return jnp.einsum('hqk,khd->qhd', probability, value_seq, precision=exact_precision)

    def by_sequence(values):
        return jnp.transpose(values.reshape(SEQ_LEN, SEQS, HEADS, HEAD_DIM), (1, 0, 2, 3))
    head_outputs = lax.map(jax.checkpoint(attend), (by_sequence(projected_queries), by_sequence(projected_keys), by_sequence(projected_values), segments.T))
    head_outputs = jnp.transpose(head_outputs, (1, 0, 2, 3)).reshape(SEQ_LEN, SEQS, INNER)
    head_outputs = reduced_precision(reduced_precision_reverse(head_outputs))
    attention_result = reduced_precision_reverse(jnp.einsum('awb,bk->awk', head_outputs, output_projection_matrix, precision=exact_precision))
    mixed = tokens + attention_result
    normed_two = reduced_precision(mixed * rms_scale(mixed) * second_gain)
    logits = reduced_precision_reverse(jnp.einsum('lsd,de->lse', normed_two, router_weight, precision=exact_precision))
    largest_logit = lax.optimization_barrier(jnp.max(logits, axis=-1, keepdims=True))
    router_exp = jnp.exp(logits - largest_logit)
    router_probs = router_exp / lax.optimization_barrier(jnp.sum(router_exp, axis=-1, keepdims=True))
    kept_mask = capacity_slot >= 0
    chosen = (routes[..., None] == jnp.arange(EXPERTS, dtype=jnp.int32)).astype(jnp.float32)
    gate_value = lax.optimization_barrier(jnp.sum(router_probs * chosen, axis=-1)) * kept_mask.astype(jnp.float32)
    sent_rows = reduced_precision_reverse(normed_two).reshape(SEQ_LEN * SEQS, D)
    rows_per = N_TENSOR * N_DP * CAP
    position = jnp.arange(SEQ_LEN, dtype=jnp.int32)[:, None]
    sequence = jnp.arange(SEQS, dtype=jnp.int32)[None, :]
    source_device = position // (SEQ_LEN // N_TENSOR) * N_DP + sequence // SEQ_DEV
    target = jnp.where(kept_mask, routes * rows_per + source_device * CAP + capacity_slot, EXPERTS * rows_per).reshape(-1).astype(jnp.int32)
    owner_row = jnp.full((EXPERTS * rows_per + 1,), -1, jnp.int32).at[target].set(jnp.arange(SEQ_LEN * SEQS, dtype=jnp.int32))[:-1]
    buffers = jnp.where((owner_row >= 0)[:, None], sent_rows[jnp.maximum(owner_row, 0)], 0.0).reshape(EXPERTS, rows_per, D)
    results = lax.map(jax.checkpoint(expert_apply), (buffers, expert_in, expert_out)).reshape(EXPERTS * rows_per, D)
    combined = jnp.where(kept_mask.reshape(-1)[:, None], results[jnp.minimum(target, EXPERTS * rows_per - 1)], 0.0)
    combined = combined.reshape(SEQ_LEN, SEQS, D)
    return mixed + gate_value[..., None] * combined

def reference(tokens, cotangent, segments, routes, capacity_slot, bucket_index, first_gain, query_projection_matrix, key_projection_matrix, value_projection_matrix, output_projection_matrix, position_bias, second_gain, router_weight, expert_in, expert_out):

    def forward(tokens_f, first_f, query_f, key_f, value_f, output_f, bias_f, second_f, router_f, in_f, out_f):
        return layer(segments, routes, capacity_slot, bucket_index, tokens_f, first_f, query_f, key_f, value_f, output_f, bias_f, second_f, router_f, in_f, out_f)
    result, pullback = jax.vjp(forward, tokens.astype(jnp.float32), first_gain.astype(jnp.float32), query_projection_matrix.astype(jnp.float32), key_projection_matrix.astype(jnp.float32), value_projection_matrix.astype(jnp.float32), output_projection_matrix.astype(jnp.float32), position_bias.astype(jnp.float32), second_gain.astype(jnp.float32), router_weight.astype(jnp.float32), expert_in.astype(jnp.float32), expert_out.astype(jnp.float32))
    grads = pullback(cotangent.astype(jnp.float32))
    return (result.astype(jnp.bfloat16), grads[0].astype(jnp.bfloat16), grads[1], grads[2], grads[3], grads[4], grads[5], grads[6], grads[7], grads[8], grads[9], grads[10])
```

```python
import jax
import jax.numpy as jnp
from jax import lax
from jax.experimental import pallas as pl
from jax.experimental.pallas import tpu as pltpu
from jax.sharding import PartitionSpec as P

HEAD_DIM = 64


epsilon = 1e-06
masked_score = -1e30
exact_precision = lax.Precision.HIGHEST
BLOCK_ROWS = 256


def rms_scale(values):
    return lax.rsqrt(jnp.mean(values * values, axis=-1, keepdims=True) + epsilon)


def smooth_gate(values):
    return jax.nn.gelu(values, approximate=True)


def mesh_split(values):
    parts = []
    for _ in range(3):
        part = values.astype(jnp.bfloat16)
        parts.append(part)
        values = values - part.astype(jnp.float32)
    return parts


def with_parts(base, lane_in_half, values):
    for place, part in enumerate(mesh_split(values)):
        base = jnp.where(lane_in_half == 8 + place, part, base)
    return base


def attention_forward(query_ref, key_ref, value_ref, penalty_ref, marks_ref, line_ref,
                      out_ref, query_out_ref, tile_ref):
    seq_len = query_ref.shape[0]
    rows = tile_ref.shape[0]
    lane = lax.broadcasted_iota(jnp.int32, (seq_len, 128), 1)
    block_lane = lax.broadcasted_iota(jnp.int32, (rows, 128), 1)
    for head in range(2):
        own = (lane < HEAD_DIM) if head == 0 else (lane >= HEAD_DIM)
        own_block = (block_lane < HEAD_DIM) if head == 0 else (block_lane >= HEAD_DIM)
        lane_in_half = jnp.where(own_block, -1, block_lane % HEAD_DIM)
        tile_ref[...] = pltpu.roll(
            jnp.broadcast_to(line_ref[0, head : head + 1, :], (rows, 2 * seq_len)),
            0, 1, stride=1, stride_axis=0,
        )
        keys = jnp.where(own, key_ref[...], marks_ref[...])
        values = value_ref[...]
        for block in range(seq_len // rows):
            part = slice(block * rows, (block + 1) * rows)
            first = seq_len - block * rows
            queries = jnp.where(
                own_block, query_ref[part, :] * HEAD_DIM ** (-0.5), penalty_ref[part, :]
            ).astype(jnp.bfloat16)
            scores = lax.dot_general(
                queries, keys, (((1,), (1,)), ((), ())), preferred_element_type=jnp.float32
            ) + tile_ref[:, first : first + seq_len]
            largest = jnp.max(scores, axis=-1, keepdims=True)
            weights = jnp.exp(scores - largest)
            total = jnp.sum(weights, axis=-1, keepdims=True)
            result = jnp.dot(
                weights.astype(jnp.bfloat16), values, preferred_element_type=jnp.float32
            ) / total
            result = result.astype(jnp.bfloat16)
            if head == 0:
                out_ref[part, :] = result
            else:
                out_ref[part, :] = jnp.where(own_block, result, out_ref[part, :])
            query_out_ref[head, part, :] = with_parts(
                queries, lane_in_half, largest + jnp.log(total)
            )


def attention_backward(query_ref, key_ref, value_ref, marks_ref, out_ref, grad_ref, line_ref,
                       grad_out_ref, line_out_ref, tile_ref, line_grad_ref, grad_query_ref):
    seq_len = key_ref.shape[0]
    rows = tile_ref.shape[0]
    inner = grad_out_ref.shape[1] // 3
    pair = pl.program_id(0)
    lane = lax.broadcasted_iota(jnp.int32, (seq_len, 128), 1)
    block_lane = lax.broadcasted_iota(jnp.int32, (rows, 128), 1)
    query_columns = pl.ds(pl.multiple_of(pair * 128, 128), 128)
    key_columns = pl.ds(pl.multiple_of(inner + pair * 128, 128), 128)
    value_columns = pl.ds(pl.multiple_of(2 * inner + pair * 128, 128), 128)
    for head in range(2):
        own = (lane < HEAD_DIM) if head == 0 else (lane >= HEAD_DIM)
        own_block = (block_lane < HEAD_DIM) if head == 0 else (block_lane >= HEAD_DIM)
        lane_in_half = jnp.where(own, -1, lane % HEAD_DIM)
        tile_ref[...] = pltpu.roll(
            jnp.broadcast_to(line_ref[0, head : head + 1, :], (rows, 2 * seq_len)),
            0, 1, stride=1, stride_axis=0,
        )
        line_grad_ref[...] = jnp.zeros_like(line_grad_ref)
        queries = query_ref[head]
        grads = jnp.where(own, grad_ref[...], jnp.zeros_like(grad_ref))
        row_term = jnp.sum(
            grads.astype(jnp.float32) * out_ref[...].astype(jnp.float32), axis=-1, keepdims=True
        )
        grads = with_parts(grads, lane_in_half, row_term)
        for block in range(seq_len // rows):
            part = slice(block * rows, (block + 1) * rows)
            first = seq_len - block * rows
            keys = jnp.where(own_block, key_ref[part, :], marks_ref[part, :])
            values = jnp.where(own_block, value_ref[part, :], marks_ref[part, :])
            scores = lax.dot_general(
                keys, queries, (((1,), (1,)), ((), ())), preferred_element_type=jnp.float32
            ) + tile_ref[:, first : first + seq_len]
            probability = jnp.exp(scores)
            grad_scores = probability * lax.dot_general(
                values, grads, (((1,), (1,)), ((), ())), preferred_element_type=jnp.float32
            )
            line_grad_ref[:, first : first + seq_len] += grad_scores
            grad_scores = grad_scores.astype(jnp.bfloat16)
            grad_value = jnp.dot(
                probability.astype(jnp.bfloat16), grads, preferred_element_type=jnp.float32
            ).astype(jnp.bfloat16)
            grad_key = jnp.dot(
                grad_scores, queries, preferred_element_type=jnp.float32
            ).astype(jnp.bfloat16)
            grad_query = lax.dot_general(
                grad_scores, keys, (((0,), (0,)), ((), ())), preferred_element_type=jnp.float32
            )
            if block == 0:
                grad_query_ref[...] = grad_query
            else:
                grad_query_ref[...] += grad_query
            if head == 1:
                grad_key = jnp.where(own_block, grad_key, grad_out_ref[part, key_columns])
                grad_value = jnp.where(own_block, grad_value, grad_out_ref[part, value_columns])
            grad_out_ref[part, key_columns] = grad_key
            grad_out_ref[part, value_columns] = grad_value
        grad_query = (grad_query_ref[...] * HEAD_DIM ** (-0.5)).astype(jnp.bfloat16)
        if head == 1:
            grad_query = jnp.where(own, grad_query, grad_out_ref[:, query_columns])
        grad_out_ref[:, query_columns] = grad_query
        folded = line_grad_ref[...]
        while folded.shape[0] > 1:
            half = folded.shape[0] // 2
            folded = folded[:half] + pltpu.roll(folded[half:], 2 * seq_len - half, 1)
        line_out_ref[0, head : head + 1, :] = folded


def local(
    tokens,
    cotangent,
    segments,
    routes,
    capacity_slot,
    bucket_index,
    first_gain,
    query_projection_matrix,
    key_projection_matrix,
    value_projection_matrix,
    output_projection_matrix,
    position_bias,
    second_gain,
    router_weight,
    expert_in,
    expert_out,
):
    half_len, seq_count, model_width = tokens.shape
    tensor_count = lax.axis_size("tensor")
    seq_len = half_len * tensor_count
    owner_count = lax.axis_size("dp")
    local_inner = query_projection_matrix.shape[1]
    head_count = local_inner // HEAD_DIM
    expert_count = router_weight.shape[1]
    token_count = half_len * seq_count
    capacity = max(2, token_count * 5 // (4 * expert_count))
    pair_count = head_count // 2
    inputs = tokens.astype(jnp.float32)
    first_scale = rms_scale(inputs)
    gain_one = first_gain.astype(jnp.float32)
    normalized_rows = (inputs * first_scale * gain_one).astype(jnp.bfloat16)
    complete_rows = lax.all_gather(normalized_rows, "tensor", axis=0, tiled=True)
    merged_heads = jnp.concatenate(
        [query_projection_matrix, key_projection_matrix, value_projection_matrix], axis=1
    )
    projected = jnp.einsum(
        "cjt,tm->cjm", complete_rows, merged_heads, preferred_element_type=jnp.float32
    ).astype(jnp.bfloat16)
    projected = projected.reshape(seq_len, 3 * local_inner)
    bucket_line = jnp.pad(bucket_index, (1, 0))
    bucket_back = jnp.pad(bucket_index[::-1], (1, 0))
    bucket_ids = jnp.arange(position_bias.shape[0], dtype=jnp.int32)[None, :]
    both_lines = jnp.dot(
        position_bias.T,
        (jnp.concatenate([bucket_line, bucket_back])[:, None] == bucket_ids).astype(jnp.bfloat16).T,
        preferred_element_type=jnp.float32,
    )
    forward_line = both_lines[:, : 2 * seq_len].reshape(pair_count, 2, 2 * seq_len)
    backward_line = both_lines[:, 2 * seq_len :].reshape(pair_count, 2, 2 * seq_len)
    lane_place = (jnp.arange(128, dtype=jnp.int32) % HEAD_DIM)[None, :]
    same_doc = segments == lane_place
    penalty = jnp.where(same_doc | (lane_place >= 8), 0.0, masked_score).astype(jnp.bfloat16)
    marks = jnp.where(
        lane_place < 8,
        same_doc.astype(jnp.float32),
        jnp.where(lane_place < 11, -1.0, 0.0),
    ).astype(jnp.bfloat16)
    block_rows = min(BLOCK_ROWS, seq_len)

    def columns(group):
        return pl.BlockSpec((seq_len, 128), lambda pair: (0, group * pair_count + pair))

    whole_block = pl.BlockSpec((seq_len, 128), lambda pair: (0, 0))
    line_block = pl.BlockSpec((1, 2, 2 * seq_len), lambda pair: (pair, 0, 0))
    query_block = pl.BlockSpec((2, seq_len, 128), lambda pair: (pair, 0, 0))
    tile_shape = pltpu.VMEM((block_rows, 2 * seq_len), jnp.float32)
    head_outputs, query_rows = pl.pallas_call(
        attention_forward,
        grid=(pair_count,),
        in_specs=[columns(0), columns(1), columns(2), whole_block, whole_block, line_block],
        out_specs=[columns(0), query_block],
        out_shape=[
            jax.ShapeDtypeStruct((seq_len, local_inner), jnp.bfloat16),
            jax.ShapeDtypeStruct((head_count, seq_len, 128), jnp.bfloat16),
        ],
        scratch_shapes=[tile_shape],
        compiler_params=pltpu.CompilerParams(vmem_limit_bytes=48 << 20),
    )(projected, projected, projected, penalty, marks, forward_line)
    head_outputs = head_outputs.reshape(seq_len, seq_count, local_inner)
    row_portion = head_outputs
    attention_result = lax.psum_scatter(
        jnp.einsum(
            "awb,bk->awk", row_portion, output_projection_matrix, preferred_element_type=jnp.float32
        ),
        "tensor",
        scatter_dimension=0,
        tiled=True,
    )
    mixed = inputs + attention_result
    second_scale = rms_scale(mixed)
    gain_two = second_gain.astype(jnp.float32)
    normed_two = (mixed * second_scale * gain_two).astype(jnp.bfloat16)
    normed_flat = normed_two.reshape(token_count, model_width)
    logits = jnp.dot(normed_flat, router_weight, preferred_element_type=jnp.float32)
    largest_logit = jnp.max(logits, axis=-1, keepdims=True)
    router_exp = jnp.exp(logits - largest_logit)
    router_probs = router_exp / jnp.sum(router_exp, axis=-1, keepdims=True)
    route_flat = routes.reshape(-1)
    slot_flat = capacity_slot.reshape(-1)
    kept_mask = slot_flat >= 0
    kept_float = kept_mask.astype(jnp.float32)
    route_hot = (route_flat[:, None] == jnp.arange(expert_count, dtype=jnp.int32)[None, :]).astype(
        jnp.float32
    )
    route_prob = jnp.sum(router_probs * route_hot, axis=-1)
    gate_value = route_prob * kept_float
    target = jnp.where(kept_mask, route_flat * capacity + slot_flat, expert_count * capacity)
    pack_hot = (
        jnp.arange(expert_count * capacity, dtype=jnp.int32)[:, None] == target[None, :]
    ).astype(jnp.bfloat16)

    first_matrix = expert_in[0]
    second_matrix = expert_out[0]
    grad_out = cotangent.astype(jnp.float32).reshape(token_count, model_width)
    grad_result = (gate_value[:, None] * grad_out).astype(jnp.bfloat16)
    packed = jnp.dot(
        pack_hot,
        jnp.concatenate([normed_flat, grad_result], axis=1),
        preferred_element_type=jnp.float32,
    ).astype(jnp.bfloat16)
    arrived = lax.all_to_all(
        packed.reshape(expert_count, capacity, 2 * model_width),
        "dp",
        split_axis=0,
        concat_axis=0,
        tiled=True,
    )
    all_rows = lax.all_gather(arrived, "tensor", axis=0, tiled=True).reshape(-1, 2 * model_width)
    expert_rows = all_rows[:, :model_width]
    grad_rows_all = all_rows[:, model_width:]
    pre_act = jnp.dot(expert_rows, first_matrix, preferred_element_type=jnp.float32)
    hidden = smooth_gate(pre_act).astype(jnp.bfloat16)
    grad_hidden = jnp.dot(grad_rows_all, second_matrix.T, preferred_element_type=jnp.float32)
    gelu_value, gelu_pull = jax.vjp(smooth_gate, pre_act)
    grad_pre = gelu_pull(grad_hidden)[0].astype(jnp.bfloat16)
    expert_result = jnp.dot(hidden, second_matrix, preferred_element_type=jnp.float32)
    grad_sent = jnp.dot(grad_pre, first_matrix.T, preferred_element_type=jnp.float32)
    summed = lax.psum_scatter(
        jnp.concatenate([expert_result.astype(jnp.bfloat16), grad_sent.astype(jnp.bfloat16)], axis=1),
        "tensor",
        scatter_dimension=0,
        tiled=True,
    )
    returned = lax.all_to_all(
        summed.reshape(owner_count, capacity, 2 * model_width),
        "dp",
        split_axis=0,
        concat_axis=0,
        tiled=True,
    ).reshape(expert_count * capacity, 2 * model_width)
    grad_second = jnp.dot(hidden.T, grad_rows_all, preferred_element_type=jnp.float32)
    grad_first = jnp.dot(expert_rows.T, grad_pre, preferred_element_type=jnp.float32)
    unpacked = lax.dot_general(
        pack_hot, returned, (((0,), (0,)), ((), ())), preferred_element_type=jnp.float32
    )
    expert_tokens = unpacked[:, :model_width]
    mixed_flat = mixed.reshape(token_count, model_width)
    layer_out = (
        (mixed_flat + gate_value[:, None] * expert_tokens)
        .astype(jnp.bfloat16)
        .reshape(half_len, seq_count, model_width)
    )
    grad_gate = jnp.sum(grad_out * expert_tokens, axis=-1)
    grad_normed_two = unpacked[:, model_width:]
    grad_kept = grad_gate * kept_float
    grad_logits = (router_probs * (route_hot - route_prob[:, None]) * grad_kept[:, None]).astype(
        jnp.bfloat16
    )
    router_part = jnp.dot(normed_flat.T, grad_logits, preferred_element_type=jnp.float32)
    grad_normed_two = grad_normed_two + jnp.dot(
        grad_logits, router_weight.T, preferred_element_type=jnp.float32
    )
    scale_flat = second_scale.reshape(token_count, 1)
    second_part = jnp.sum(grad_normed_two * mixed_flat * scale_flat, axis=0)
    scaled_two = grad_normed_two * gain_two
    grad_mixed = (
        grad_out
        + scale_flat * scaled_two
        - mixed_flat
        * scale_flat
        * scale_flat
        * scale_flat
        * jnp.mean(mixed_flat * scaled_two, axis=-1, keepdims=True)
    )
    grad_attended = grad_mixed.astype(jnp.bfloat16).reshape(half_len, seq_count, model_width)
    gradient_attention_total = lax.all_gather(grad_attended, "tensor", axis=0, tiled=True)
    output_part = jnp.einsum(
        "bkn,bkx->nx", head_outputs, gradient_attention_total, preferred_element_type=jnp.float32
    )
    grad_heads = jnp.einsum(
        "zur,yr->zuy",
        gradient_attention_total,
        output_projection_matrix,
        preferred_element_type=jnp.float32,
    ).astype(jnp.bfloat16)
    grad_heads = grad_heads.reshape(seq_len, local_inner)
    gradient_merged_heads, line_grad = pl.pallas_call(
        attention_backward,
        grid=(pair_count,),
        in_specs=[
            query_block,
            columns(1),
            columns(2),
            whole_block,
            columns(0),
            columns(0),
            line_block,
        ],
        out_specs=[
            pl.BlockSpec((seq_len, 3 * local_inner), lambda pair: (0, 0)),
            line_block,
        ],
        out_shape=[
            jax.ShapeDtypeStruct((seq_len, 3 * local_inner), jnp.bfloat16),
            jax.ShapeDtypeStruct((pair_count, 2, 2 * seq_len), jnp.float32),
        ],
        scratch_shapes=[
            tile_shape,
            tile_shape,
            pltpu.VMEM((seq_len, 128), jnp.float32),
        ],
        compiler_params=pltpu.CompilerParams(vmem_limit_bytes=48 << 20),
    )(
        query_rows,
        projected,
        projected,
        marks,
        head_outputs.reshape(seq_len, local_inner),
        grad_heads,
        backward_line,
    )
    gradient_merged_heads = gradient_merged_heads.reshape(seq_len, seq_count, 3 * local_inner)
    bias_part_total = jnp.dot(
        (bucket_back[:, None] == bucket_ids).astype(jnp.float32).T,
        line_grad.reshape(head_count, 2 * seq_len).T,
        precision=exact_precision,
    )
    joined_part = jnp.einsum(
        "mtu,mtj->uj", complete_rows, gradient_merged_heads, preferred_element_type=jnp.float32
    )
    row_portion = gradient_merged_heads
    grad_normed = lax.psum_scatter(
        jnp.einsum(
            "ybq,gq->ybg", row_portion, merged_heads, preferred_element_type=jnp.float32
        ).astype(jnp.bfloat16),
        "tensor",
        scatter_dimension=0,
        tiled=True,
    ).astype(jnp.float32)
    first_part = jnp.sum(grad_normed * inputs * first_scale, axis=(0, 1))
    scaled_one = grad_normed * gain_one
    grad_mixed_grid = grad_mixed.reshape(half_len, seq_count, model_width)
    tokens_grad = (
        grad_mixed_grid
        + first_scale * scaled_one
        - inputs
        * first_scale
        * first_scale
        * first_scale
        * jnp.mean(inputs * scaled_one, axis=-1, keepdims=True)
    )
    output_grad = lax.psum(output_part.astype(jnp.bfloat16), "dp").astype(jnp.float32)
    joined_grad = lax.psum(joined_part.astype(jnp.bfloat16), "dp").astype(jnp.float32)
    query_grad = joined_grad[:, :local_inner]
    key_grad = joined_grad[:, local_inner : 2 * local_inner]
    value_grad = joined_grad[:, 2 * local_inner :]
    bias_rows = jnp.zeros((tensor_count,) + bias_part_total.shape, jnp.float32)
    bias_rows = lax.dynamic_update_index_in_dim(
        bias_rows, bias_part_total, lax.axis_index("tensor"), 0
    )
    small_sizes = [router_part.size, model_width, model_width]
    small = lax.psum(
        jnp.concatenate([router_part.reshape(-1), first_part, second_part, bias_rows.reshape(-1)]),
        ("dp", "tensor"),
    )
    router_grad = small[: small_sizes[0]].reshape(router_part.shape)
    first_gain_grad = small[small_sizes[0] : small_sizes[0] + model_width]
    second_gain_grad = small[small_sizes[0] + model_width : small_sizes[0] + 2 * model_width]
    position_bias_grad = lax.dynamic_index_in_dim(
        small[small_sizes[0] + 2 * model_width :].reshape(bias_rows.shape),
        lax.axis_index("tensor"),
        0,
        keepdims=False,
    )
    return (
        layer_out,
        tokens_grad.astype(jnp.bfloat16),
        first_gain_grad,
        query_grad,
        key_grad,
        value_grad,
        output_grad,
        position_bias_grad,
        second_gain_grad,
        router_grad,
        grad_first[None],
        grad_second[None],
    )


def solution(mesh):
    return jax.shard_map(
        local,
        mesh=mesh,
        in_specs=(
            P("tensor", "dp", None),
            P("tensor", "dp", None),
            P(None, "dp"),
            P("tensor", "dp"),
            P("tensor", "dp"),
            P(),
            P(),
            P(None, "tensor"),
            P(None, "tensor"),
            P(None, "tensor"),
            P("tensor", None),
            P(None, "tensor"),
            P(),
            P(),
            P("dp", None, "tensor"),
            P("dp", "tensor", None),
        ),
        out_specs=(
            P("tensor", "dp", None),
            P("tensor", "dp", None),
            P(),
            P(None, "tensor"),
            P(None, "tensor"),
            P(None, "tensor"),
            P("tensor", None),
            P(None, "tensor"),
            P(),
            P(),
            P("dp", None, "tensor"),
            P("dp", "tensor", None),
        ),
        check_vma=False,
    )
```

```python
import jax
import jax.numpy as jnp
from jax import lax
from jax.experimental import pallas as pl
from jax.experimental.pallas import tpu as pltpu
from jax.sharding import PartitionSpec as P

HEAD_DIM = 64


epsilon = 1e-06
masked_score = -1e30
exact_precision = lax.Precision.HIGHEST
BLOCK_ROWS = 256


def rms_scale(values):
    return lax.rsqrt(jnp.mean(values * values, axis=-1, keepdims=True) + epsilon)


def smooth_gate(values):
    return jax.nn.gelu(values, approximate=True)


def mesh_split(values):
    parts = []
    for _ in range(3):
        part = values.astype(jnp.bfloat16)
        parts.append(part)
        values = values - part.astype(jnp.float32)
    return parts


def with_parts(base, lane_in_half, values):
    for place, part in enumerate(mesh_split(values)):
        base = jnp.where(lane_in_half == 8 + place, part, base)
    return base


def attention_forward(query_ref, key_ref, value_ref, penalty_ref, marks_ref, line_ref,
                      out_ref, query_out_ref, tile_ref):
    seq_len = query_ref.shape[0]
    rows = tile_ref.shape[0]
    lane = lax.broadcasted_iota(jnp.int32, (seq_len, 128), 1)
    block_lane = lax.broadcasted_iota(jnp.int32, (rows, 128), 1)
    for head in range(2):
        own = (lane < HEAD_DIM) if head == 0 else (lane >= HEAD_DIM)
        own_block = (block_lane < HEAD_DIM) if head == 0 else (block_lane >= HEAD_DIM)
        lane_in_half = jnp.where(own_block, -1, block_lane % HEAD_DIM)
        tile_ref[...] = pltpu.roll(
            jnp.broadcast_to(line_ref[0, head : head + 1, :], (rows, 2 * seq_len)),
            0, 1, stride=1, stride_axis=0,
        )
        keys = jnp.where(own, key_ref[...], marks_ref[...])
        values = value_ref[...]
        for block in range(seq_len // rows):
            part = slice(block * rows, (block + 1) * rows)
            first = seq_len - block * rows
            queries = jnp.where(
                own_block, query_ref[part, :] * HEAD_DIM ** (-0.5), penalty_ref[part, :]
            ).astype(jnp.bfloat16)
            scores = lax.dot_general(
                queries, keys, (((1,), (1,)), ((), ())), preferred_element_type=jnp.float32
            ) + tile_ref[:, first : first + seq_len]
            largest = jnp.max(scores, axis=-1, keepdims=True)
            weights = jnp.exp(scores - largest)
            total = jnp.sum(weights, axis=-1, keepdims=True)
            result = jnp.dot(
                weights.astype(jnp.bfloat16), values, preferred_element_type=jnp.float32
            ) / total
            result = result.astype(jnp.bfloat16)
            if head == 0:
                out_ref[part, :] = result
            else:
                out_ref[part, :] = jnp.where(own_block, result, out_ref[part, :])
            query_out_ref[head, part, :] = with_parts(
                queries, lane_in_half, largest + jnp.log(total)
            )


def attention_backward(query_ref, key_ref, value_ref, marks_ref, out_ref, grad_ref, line_ref,
                       grad_out_ref, line_out_ref, tile_ref, line_grad_ref, grad_query_ref):
    seq_len = key_ref.shape[0]
    rows = tile_ref.shape[0]
    inner = grad_out_ref.shape[1] // 3
    pair = pl.program_id(0)
    lane = lax.broadcasted_iota(jnp.int32, (seq_len, 128), 1)
    block_lane = lax.broadcasted_iota(jnp.int32, (rows, 128), 1)
    query_columns = pl.ds(pl.multiple_of(pair * 128, 128), 128)
    key_columns = pl.ds(pl.multiple_of(inner + pair * 128, 128), 128)
    value_columns = pl.ds(pl.multiple_of(2 * inner + pair * 128, 128), 128)
    for head in range(2):
        own = (lane < HEAD_DIM) if head == 0 else (lane >= HEAD_DIM)
        own_block = (block_lane < HEAD_DIM) if head == 0 else (block_lane >= HEAD_DIM)
        lane_in_half = jnp.where(own, -1, lane % HEAD_DIM)
        tile_ref[...] = pltpu.roll(
            jnp.broadcast_to(line_ref[0, head : head + 1, :], (rows, 2 * seq_len)),
            0, 1, stride=1, stride_axis=0,
        )
        line_grad_ref[...] = jnp.zeros_like(line_grad_ref)
        queries = query_ref[head]
        grads = jnp.where(own, grad_ref[...], jnp.zeros_like(grad_ref))
        row_term = jnp.sum(
            grads.astype(jnp.float32) * out_ref[...].astype(jnp.float32), axis=-1, keepdims=True
        )
        grads = with_parts(grads, lane_in_half, row_term)
        for block in range(seq_len // rows):
            part = slice(block * rows, (block + 1) * rows)
            first = seq_len - block * rows
            keys = jnp.where(own_block, key_ref[part, :], marks_ref[part, :])
            values = jnp.where(own_block, value_ref[part, :], marks_ref[part, :])
            scores = lax.dot_general(
                keys, queries, (((1,), (1,)), ((), ())), preferred_element_type=jnp.float32
            ) + tile_ref[:, first : first + seq_len]
            probability = jnp.exp(scores)
            grad_scores = probability * lax.dot_general(
                values, grads, (((1,), (1,)), ((), ())), preferred_element_type=jnp.float32
            )
            line_grad_ref[:, first : first + seq_len] += grad_scores
            grad_scores = grad_scores.astype(jnp.bfloat16)
            grad_value = jnp.dot(
                probability.astype(jnp.bfloat16), grads, preferred_element_type=jnp.float32
            ).astype(jnp.bfloat16)
            grad_key = jnp.dot(
                grad_scores, queries, preferred_element_type=jnp.float32
            ).astype(jnp.bfloat16)
            grad_query = lax.dot_general(
                grad_scores, keys, (((0,), (0,)), ((), ())), preferred_element_type=jnp.float32
            )
            if block == 0:
                grad_query_ref[...] = grad_query
            else:
                grad_query_ref[...] += grad_query
            if head == 1:
                grad_key = jnp.where(own_block, grad_key, grad_out_ref[part, key_columns])
                grad_value = jnp.where(own_block, grad_value, grad_out_ref[part, value_columns])
            grad_out_ref[part, key_columns] = grad_key
            grad_out_ref[part, value_columns] = grad_value
        grad_query = (grad_query_ref[...] * HEAD_DIM ** (-0.5)).astype(jnp.bfloat16)
        if head == 1:
            grad_query = jnp.where(own, grad_query, grad_out_ref[:, query_columns])
        grad_out_ref[:, query_columns] = grad_query
        folded = line_grad_ref[...]
        while folded.shape[0] > 1:
            half = folded.shape[0] // 2
            folded = folded[:half] + pltpu.roll(folded[half:], 2 * seq_len - half, 1)
        line_out_ref[0, head : head + 1, :] = folded


def exchange(values, bit):
    count = lax.axis_size("dp")
    return lax.ppermute(values, "dp", [(i, i ^ (1 << bit)) for i in range(count)])


def exchange_sum(values):
    for bit in range(lax.axis_size("dp").bit_length() - 1):
        values = values + exchange(values, bit)
    return values


def halving_sum(values, turn):
    bit_count = lax.axis_size("dp").bit_length() - 1
    position = lax.axis_index("dp")
    width = values.shape[1]
    order = [(step + turn) % bit_count for step in range(bit_count)]
    total = values
    for bit in order:
        halves = total.reshape(2, total.shape[0] // 2, width)
        mine = (position >> bit) & 1
        theirs = lax.dynamic_index_in_dim(halves, 1 - mine, 0, keepdims=False)
        kept = lax.dynamic_index_in_dim(halves, mine, 0, keepdims=False)
        arrived = exchange(theirs.astype(jnp.bfloat16), bit)
        total = kept.astype(jnp.float32) + arrived.astype(jnp.float32)
    total = total.astype(jnp.bfloat16)
    for bit in reversed(order):
        mine = (position >> bit) & 1
        rows = total.shape[0]
        arrived = exchange(total, bit)
        whole = jnp.zeros((2 * rows, width), total.dtype)
        whole = lax.dynamic_update_slice_in_dim(whole, arrived, (1 - mine) * rows, 0)
        total = lax.dynamic_update_slice_in_dim(whole, total, mine * rows, 0)
    return total.astype(jnp.float32)


def local(
    tokens,
    cotangent,
    segments,
    routes,
    capacity_slot,
    bucket_index,
    first_gain,
    query_projection_matrix,
    key_projection_matrix,
    value_projection_matrix,
    output_projection_matrix,
    position_bias,
    second_gain,
    router_weight,
    expert_in,
    expert_out,
):
    half_len, seq_count, model_width = tokens.shape
    tensor_count = lax.axis_size("tensor")
    seq_len = half_len * tensor_count
    owner_count = lax.axis_size("dp")
    local_inner = query_projection_matrix.shape[1]
    head_count = local_inner // HEAD_DIM
    expert_count = router_weight.shape[1]
    token_count = half_len * seq_count
    capacity = max(2, token_count * 5 // (4 * expert_count))
    pair_count = head_count // 2
    inputs = tokens.astype(jnp.float32)
    first_scale = rms_scale(inputs)
    gain_one = first_gain.astype(jnp.float32)
    normalized_rows = (inputs * first_scale * gain_one).astype(jnp.bfloat16)
    place = lax.axis_index("tensor")
    own_start = place * half_len
    other_start = half_len - own_start

    def swap(values):
        return lax.ppermute(values, "tensor", [(0, 1), (1, 0)])

    def gather_rows(values):
        whole = jnp.zeros((seq_len,) + values.shape[1:], values.dtype)
        whole = lax.dynamic_update_slice_in_dim(whole, swap(values), other_start, 0)
        return lax.dynamic_update_slice_in_dim(whole, values, own_start, 0)

    def scatter_rows(rows, multiply):
        theirs = multiply(lax.dynamic_slice_in_dim(rows, other_start, half_len, 0))
        received = swap(theirs.astype(jnp.bfloat16))
        own = multiply(lax.dynamic_slice_in_dim(rows, own_start, half_len, 0))
        return own + received.astype(jnp.float32)

    complete_rows = gather_rows(normalized_rows)
    merged_heads = jnp.concatenate(
        [query_projection_matrix, key_projection_matrix, value_projection_matrix], axis=1
    )
    projected = jnp.einsum(
        "cjt,tm->cjm", complete_rows, merged_heads, preferred_element_type=jnp.float32
    ).astype(jnp.bfloat16)
    projected = projected.reshape(seq_len, 3 * local_inner)
    bucket_line = jnp.pad(bucket_index, (1, 0))
    bucket_back = jnp.pad(bucket_index[::-1], (1, 0))
    bucket_ids = jnp.arange(position_bias.shape[0], dtype=jnp.int32)[None, :]
    both_lines = jnp.dot(
        position_bias.T,
        (jnp.concatenate([bucket_line, bucket_back])[:, None] == bucket_ids).astype(jnp.bfloat16).T,
        preferred_element_type=jnp.float32,
    )
    forward_line = both_lines[:, : 2 * seq_len].reshape(pair_count, 2, 2 * seq_len)
    backward_line = both_lines[:, 2 * seq_len :].reshape(pair_count, 2, 2 * seq_len)
    lane_place = (jnp.arange(128, dtype=jnp.int32) % HEAD_DIM)[None, :]
    same_doc = segments == lane_place
    penalty = jnp.where(same_doc | (lane_place >= 8), 0.0, masked_score).astype(jnp.bfloat16)
    marks = jnp.where(
        lane_place < 8,
        same_doc.astype(jnp.float32),
        jnp.where(lane_place < 11, -1.0, 0.0),
    ).astype(jnp.bfloat16)
    block_rows = min(BLOCK_ROWS, seq_len)

    def columns(group):
        return pl.BlockSpec((seq_len, 128), lambda pair: (0, group * pair_count + pair))

    whole_block = pl.BlockSpec((seq_len, 128), lambda pair: (0, 0))
    line_block = pl.BlockSpec((1, 2, 2 * seq_len), lambda pair: (pair, 0, 0))
    query_block = pl.BlockSpec((2, seq_len, 128), lambda pair: (pair, 0, 0))
    tile_shape = pltpu.VMEM((block_rows, 2 * seq_len), jnp.float32)
    head_outputs, query_rows = pl.pallas_call(
        attention_forward,
        grid=(pair_count,),
        in_specs=[columns(0), columns(1), columns(2), whole_block, whole_block, line_block],
        out_specs=[columns(0), query_block],
        out_shape=[
            jax.ShapeDtypeStruct((seq_len, local_inner), jnp.bfloat16),
            jax.ShapeDtypeStruct((head_count, seq_len, 128), jnp.bfloat16),
        ],
        scratch_shapes=[tile_shape],
        compiler_params=pltpu.CompilerParams(vmem_limit_bytes=48 << 20),
    )(projected, projected, projected, penalty, marks, forward_line)
    head_outputs = head_outputs.reshape(seq_len, seq_count, local_inner)
    attention_result = scatter_rows(
        head_outputs,
        lambda rows: jnp.einsum(
            "awb,bk->awk", rows, output_projection_matrix, preferred_element_type=jnp.float32
        ),
    )
    mixed = inputs + attention_result
    second_scale = rms_scale(mixed)
    gain_two = second_gain.astype(jnp.float32)
    normed_two = (mixed * second_scale * gain_two).astype(jnp.bfloat16)
    normed_flat = normed_two.reshape(token_count, model_width)
    logits = jnp.dot(normed_flat, router_weight, preferred_element_type=jnp.float32)
    largest_logit = jnp.max(logits, axis=-1, keepdims=True)
    router_exp = jnp.exp(logits - largest_logit)
    router_probs = router_exp / jnp.sum(router_exp, axis=-1, keepdims=True)
    route_flat = routes.reshape(-1)
    slot_flat = capacity_slot.reshape(-1)
    kept_mask = slot_flat >= 0
    kept_float = kept_mask.astype(jnp.float32)
    route_hot = (route_flat[:, None] == jnp.arange(expert_count, dtype=jnp.int32)[None, :]).astype(
        jnp.float32
    )
    route_prob = jnp.sum(router_probs * route_hot, axis=-1)
    gate_value = route_prob * kept_float
    target = jnp.where(kept_mask, route_flat * capacity + slot_flat, expert_count * capacity)
    pack_hot = (
        jnp.arange(expert_count * capacity, dtype=jnp.int32)[:, None] == target[None, :]
    ).astype(jnp.bfloat16)

    first_matrix = expert_in[0]
    second_matrix = expert_out[0]
    grad_out = cotangent.astype(jnp.float32).reshape(token_count, model_width)
    grad_result = (gate_value[:, None] * grad_out).astype(jnp.bfloat16)
    packed = jnp.dot(
        pack_hot,
        jnp.concatenate([normed_flat, grad_result], axis=1),
        preferred_element_type=jnp.float32,
    ).astype(jnp.bfloat16)
    arrived = lax.all_to_all(
        packed.reshape(expert_count, capacity, 2 * model_width),
        "dp",
        split_axis=0,
        concat_axis=0,
        tiled=True,
    )
    arrived = arrived.reshape(-1, 2 * model_width)
    row_count = arrived.shape[0]
    all_rows = jnp.concatenate([arrived, swap(arrived)], axis=0)
    expert_rows = all_rows[:, :model_width]
    grad_rows_all = all_rows[:, model_width:]
    pre_act = jnp.dot(expert_rows, first_matrix, preferred_element_type=jnp.float32)
    hidden = smooth_gate(pre_act).astype(jnp.bfloat16)
    grad_hidden = jnp.dot(grad_rows_all, second_matrix.T, preferred_element_type=jnp.float32)
    gelu_value, gelu_pull = jax.vjp(smooth_gate, pre_act)
    grad_pre = gelu_pull(grad_hidden)[0].astype(jnp.bfloat16)

    def results(part):
        return jnp.concatenate(
            [
                jnp.dot(hidden[part], second_matrix, preferred_element_type=jnp.float32).astype(
                    jnp.bfloat16
                ),
                jnp.dot(grad_pre[part], first_matrix.T, preferred_element_type=jnp.float32).astype(
                    jnp.bfloat16
                ),
            ],
            axis=1,
        )

    received = swap(results(slice(row_count, 2 * row_count)))
    summed = results(slice(0, row_count)) + received
    returned = lax.all_to_all(
        summed.reshape(owner_count, capacity, 2 * model_width),
        "dp",
        split_axis=0,
        concat_axis=0,
        tiled=True,
    ).reshape(expert_count * capacity, 2 * model_width)
    grad_second = jnp.dot(hidden.T, grad_rows_all, preferred_element_type=jnp.float32)
    grad_first = jnp.dot(expert_rows.T, grad_pre, preferred_element_type=jnp.float32)
    unpacked = lax.dot_general(
        pack_hot, returned, (((0,), (0,)), ((), ())), preferred_element_type=jnp.float32
    )
    expert_tokens = unpacked[:, :model_width]
    mixed_flat = mixed.reshape(token_count, model_width)
    layer_out = (
        (mixed_flat + gate_value[:, None] * expert_tokens)
        .astype(jnp.bfloat16)
        .reshape(half_len, seq_count, model_width)
    )
    grad_gate = jnp.sum(grad_out * expert_tokens, axis=-1)
    grad_normed_two = unpacked[:, model_width:]
    grad_kept = grad_gate * kept_float
    grad_logits = (router_probs * (route_hot - route_prob[:, None]) * grad_kept[:, None]).astype(
        jnp.bfloat16
    )
    router_part = jnp.dot(normed_flat.T, grad_logits, preferred_element_type=jnp.float32)
    grad_normed_two = grad_normed_two + jnp.dot(
        grad_logits, router_weight.T, preferred_element_type=jnp.float32
    )
    scale_flat = second_scale.reshape(token_count, 1)
    second_part = jnp.sum(grad_normed_two * mixed_flat * scale_flat, axis=0)
    scaled_two = grad_normed_two * gain_two
    grad_mixed = (
        grad_out
        + scale_flat * scaled_two
        - mixed_flat
        * scale_flat
        * scale_flat
        * scale_flat
        * jnp.mean(mixed_flat * scaled_two, axis=-1, keepdims=True)
    )
    grad_attended = grad_mixed.astype(jnp.bfloat16).reshape(half_len, seq_count, model_width)
    gradient_attention_total = gather_rows(grad_attended)
    output_part = jnp.einsum(
        "bkn,bkx->nx", head_outputs, gradient_attention_total, preferred_element_type=jnp.float32
    )
    grad_heads = jnp.einsum(
        "zur,yr->zuy",
        gradient_attention_total,
        output_projection_matrix,
        preferred_element_type=jnp.float32,
    ).astype(jnp.bfloat16)
    grad_heads = grad_heads.reshape(seq_len, local_inner)
    gradient_merged_heads, line_grad = pl.pallas_call(
        attention_backward,
        grid=(pair_count,),
        in_specs=[
            query_block,
            columns(1),
            columns(2),
            whole_block,
            columns(0),
            columns(0),
            line_block,
        ],
        out_specs=[
            pl.BlockSpec((seq_len, 3 * local_inner), lambda pair: (0, 0)),
            line_block,
        ],
        out_shape=[
            jax.ShapeDtypeStruct((seq_len, 3 * local_inner), jnp.bfloat16),
            jax.ShapeDtypeStruct((pair_count, 2, 2 * seq_len), jnp.float32),
        ],
        scratch_shapes=[
            tile_shape,
            tile_shape,
            pltpu.VMEM((seq_len, 128), jnp.float32),
        ],
        compiler_params=pltpu.CompilerParams(vmem_limit_bytes=48 << 20),
    )(
        query_rows,
        projected,
        projected,
        marks,
        head_outputs.reshape(seq_len, local_inner),
        grad_heads,
        backward_line,
    )
    gradient_merged_heads = gradient_merged_heads.reshape(seq_len, seq_count, 3 * local_inner)
    bias_part_total = jnp.dot(
        (bucket_back[:, None] == bucket_ids).astype(jnp.float32).T,
        line_grad.reshape(head_count, 2 * seq_len).T,
        precision=exact_precision,
    )
    joined_part = jnp.einsum(
        "mtu,mtj->uj", complete_rows, gradient_merged_heads, preferred_element_type=jnp.float32
    )
    grad_normed = scatter_rows(
        gradient_merged_heads,
        lambda rows: jnp.einsum(
            "ybq,gq->ybg", rows, merged_heads, preferred_element_type=jnp.float32
        ),
    )
    first_part = jnp.sum(grad_normed * inputs * first_scale, axis=(0, 1))
    scaled_one = grad_normed * gain_one
    grad_mixed_grid = grad_mixed.reshape(half_len, seq_count, model_width)
    tokens_grad = (
        grad_mixed_grid
        + first_scale * scaled_one
        - inputs
        * first_scale
        * first_scale
        * first_scale
        * jnp.mean(inputs * scaled_one, axis=-1, keepdims=True)
    )
    early_part = jnp.concatenate([router_part.reshape(-1), second_part])
    early_grad = exchange_sum(early_part + swap(early_part))
    first_part = first_part + swap(first_part)
    late_grad = exchange_sum(jnp.concatenate([first_part, bias_part_total.reshape(-1)]))
    first_gain_grad = late_grad[:model_width]
    position_bias_grad = late_grad[model_width:].reshape(bias_part_total.shape)
    router_grad = early_grad[: router_part.size].reshape(router_part.shape)
    second_gain_grad = early_grad[router_part.size :]
    output_grad = halving_sum(output_part, 1)
    query_grad, key_grad, value_grad = [
        halving_sum(joined_part[:, group * local_inner : (group + 1) * local_inner], group)
        for group in range(3)
    ]
    return (
        layer_out,
        tokens_grad.astype(jnp.bfloat16),
        first_gain_grad,
        query_grad,
        key_grad,
        value_grad,
        output_grad,
        position_bias_grad,
        second_gain_grad,
        router_grad,
        grad_first[None],
        grad_second[None],
    )


def solution(mesh):
    return jax.shard_map(
        local,
        mesh=mesh,
        in_specs=(
            P("tensor", "dp", None),
            P("tensor", "dp", None),
            P(None, "dp"),
            P("tensor", "dp"),
            P("tensor", "dp"),
            P(),
            P(),
            P(None, "tensor"),
            P(None, "tensor"),
            P(None, "tensor"),
            P("tensor", None),
            P(None, "tensor"),
            P(),
            P(),
            P("dp", None, "tensor"),
            P("dp", "tensor", None),
        ),
        out_specs=(
            P("tensor", "dp", None),
            P("tensor", "dp", None),
            P(),
            P(None, "tensor"),
            P(None, "tensor"),
            P(None, "tensor"),
            P("tensor", None),
            P(None, "tensor"),
            P(),
            P(),
            P("dp", None, "tensor"),
            P("dp", "tensor", None),
        ),
        check_vma=False,
    )
```

```python
import jax
import jax.numpy as jnp
from jax import lax
from jax.experimental import pallas as pl
from jax.experimental.pallas import tpu as pltpu
from jax.sharding import PartitionSpec as P

HEAD_DIM = 64


epsilon = 1e-06
masked_score = -1e30
exact_precision = lax.Precision.HIGHEST
BLOCK_ROWS = 256


def rms_scale(values):
    return lax.rsqrt(jnp.mean(values * values, axis=-1, keepdims=True) + epsilon)


def smooth_gate(values):
    return jax.nn.gelu(values, approximate=True)


def mesh_split(values):
    parts = []
    for _ in range(3):
        part = values.astype(jnp.bfloat16)
        parts.append(part)
        values = values - part.astype(jnp.float32)
    return parts


def with_parts(base, lane_in_half, values):
    for place, part in enumerate(mesh_split(values)):
        base = jnp.where(lane_in_half == 8 + place, part, base)
    return base


def attention_forward(query_ref, key_ref, value_ref, penalty_ref, marks_ref, line_ref,
                      out_ref, query_out_ref, tile_ref):
    seq_len = query_ref.shape[0]
    rows = tile_ref.shape[0]
    lane = lax.broadcasted_iota(jnp.int32, (seq_len, 128), 1)
    block_lane = lax.broadcasted_iota(jnp.int32, (rows, 128), 1)
    for head in range(2):
        own = (lane < HEAD_DIM) if head == 0 else (lane >= HEAD_DIM)
        own_block = (block_lane < HEAD_DIM) if head == 0 else (block_lane >= HEAD_DIM)
        lane_in_half = jnp.where(own_block, -1, block_lane % HEAD_DIM)
        tile_ref[...] = pltpu.roll(
            jnp.broadcast_to(line_ref[0, head : head + 1, :], (rows, 2 * seq_len)),
            0, 1, stride=1, stride_axis=0,
        )
        keys = jnp.where(own, key_ref[...], marks_ref[...])
        values = value_ref[...]
        for block in range(seq_len // rows):
            part = slice(block * rows, (block + 1) * rows)
            first = seq_len - block * rows
            queries = jnp.where(
                own_block, query_ref[part, :] * HEAD_DIM ** (-0.5), penalty_ref[part, :]
            ).astype(jnp.bfloat16)
            scores = lax.dot_general(
                queries, keys, (((1,), (1,)), ((), ())), preferred_element_type=jnp.float32
            ) + tile_ref[:, first : first + seq_len]
            largest = jnp.max(scores, axis=-1, keepdims=True)
            weights = jnp.exp(scores - largest)
            total = jnp.sum(weights, axis=-1, keepdims=True)
            result = jnp.dot(
                weights.astype(jnp.bfloat16), values, preferred_element_type=jnp.float32
            ) / total
            result = result.astype(jnp.bfloat16)
            if head == 0:
                out_ref[part, :] = result
            else:
                out_ref[part, :] = jnp.where(own_block, result, out_ref[part, :])
            query_out_ref[head, part, :] = with_parts(
                queries, lane_in_half, largest + jnp.log(total)
            )


def attention_backward(query_ref, key_ref, value_ref, marks_ref, out_ref, grad_ref, line_ref,
                       grad_out_ref, line_out_ref, tile_ref, line_grad_ref, grad_query_ref):
    seq_len = key_ref.shape[0]
    rows = tile_ref.shape[0]
    inner = grad_out_ref.shape[1] // 3
    pair = pl.program_id(0)
    lane = lax.broadcasted_iota(jnp.int32, (seq_len, 128), 1)
    block_lane = lax.broadcasted_iota(jnp.int32, (rows, 128), 1)
    query_columns = pl.ds(pl.multiple_of(pair * 128, 128), 128)
    key_columns = pl.ds(pl.multiple_of(inner + pair * 128, 128), 128)
    value_columns = pl.ds(pl.multiple_of(2 * inner + pair * 128, 128), 128)
    for head in range(2):
        own = (lane < HEAD_DIM) if head == 0 else (lane >= HEAD_DIM)
        own_block = (block_lane < HEAD_DIM) if head == 0 else (block_lane >= HEAD_DIM)
        lane_in_half = jnp.where(own, -1, lane % HEAD_DIM)
        tile_ref[...] = pltpu.roll(
            jnp.broadcast_to(line_ref[0, head : head + 1, :], (rows, 2 * seq_len)),
            0, 1, stride=1, stride_axis=0,
        )
        line_grad_ref[...] = jnp.zeros_like(line_grad_ref)
        queries = query_ref[head]
        grads = jnp.where(own, grad_ref[...], jnp.zeros_like(grad_ref))
        row_term = jnp.sum(
            grads.astype(jnp.float32) * out_ref[...].astype(jnp.float32), axis=-1, keepdims=True
        )
        grads = with_parts(grads, lane_in_half, row_term)
        for block in range(seq_len // rows):
            part = slice(block * rows, (block + 1) * rows)
            first = seq_len - block * rows
            keys = jnp.where(own_block, key_ref[part, :], marks_ref[part, :])
            values = jnp.where(own_block, value_ref[part, :], marks_ref[part, :])
            scores = lax.dot_general(
                keys, queries, (((1,), (1,)), ((), ())), preferred_element_type=jnp.float32
            ) + tile_ref[:, first : first + seq_len]
            probability = jnp.exp(scores)
            grad_scores = probability * lax.dot_general(
                values, grads, (((1,), (1,)), ((), ())), preferred_element_type=jnp.float32
            )
            line_grad_ref[:, first : first + seq_len] += grad_scores
            grad_scores = grad_scores.astype(jnp.bfloat16)
            grad_value = jnp.dot(
                probability.astype(jnp.bfloat16), grads, preferred_element_type=jnp.float32
            ).astype(jnp.bfloat16)
            grad_key = jnp.dot(
                grad_scores, queries, preferred_element_type=jnp.float32
            ).astype(jnp.bfloat16)
            grad_query = lax.dot_general(
                grad_scores, keys, (((0,), (0,)), ((), ())), preferred_element_type=jnp.float32
            )
            if block == 0:
                grad_query_ref[...] = grad_query
            else:
                grad_query_ref[...] += grad_query
            if head == 1:
                grad_key = jnp.where(own_block, grad_key, grad_out_ref[part, key_columns])
                grad_value = jnp.where(own_block, grad_value, grad_out_ref[part, value_columns])
            grad_out_ref[part, key_columns] = grad_key
            grad_out_ref[part, value_columns] = grad_value
        grad_query = (grad_query_ref[...] * HEAD_DIM ** (-0.5)).astype(jnp.bfloat16)
        if head == 1:
            grad_query = jnp.where(own, grad_query, grad_out_ref[:, query_columns])
        grad_out_ref[:, query_columns] = grad_query
        folded = line_grad_ref[...]
        while folded.shape[0] > 1:
            half = folded.shape[0] // 2
            folded = folded[:half] + pltpu.roll(folded[half:], 2 * seq_len - half, 1)
        line_out_ref[0, head : head + 1, :] = folded


def exchange(values, bit):
    count = lax.axis_size("dp")
    return lax.ppermute(values, "dp", [(i, i ^ (1 << bit)) for i in range(count)])


def exchange_sum(values):
    for bit in range(lax.axis_size("dp").bit_length() - 1):
        values = values + exchange(values, bit)
    return values


def halving_steps(values, turn):
    bit_count = lax.axis_size("dp").bit_length() - 1
    position = lax.axis_index("dp")
    width = values.shape[1]
    order = [(step + turn) % bit_count for step in range(bit_count)]
    total = values
    for bit in order[:-2]:
        halves = total.reshape(2, total.shape[0] // 2, width)
        mine = (position >> bit) & 1
        theirs = lax.dynamic_index_in_dim(halves, 1 - mine, 0, keepdims=False)
        kept = lax.dynamic_index_in_dim(halves, mine, 0, keepdims=False)
        arrived = exchange(theirs.astype(jnp.bfloat16), bit)
        total = kept.astype(jnp.float32) + arrived.astype(jnp.float32)
        yield total
    total = total.astype(jnp.bfloat16)
    for bit in order[-2:]:
        total = (
            total.astype(jnp.float32) + exchange(total, bit).astype(jnp.float32)
        ).astype(jnp.bfloat16)
        yield total
    for bit in reversed(order[:-2]):
        mine = (position >> bit) & 1
        rows = total.shape[0]
        arrived = exchange(total, bit)
        whole = jnp.zeros((2 * rows, width), total.dtype)
        whole = lax.dynamic_update_slice_in_dim(whole, arrived, (1 - mine) * rows, 0)
        total = lax.dynamic_update_slice_in_dim(whole, total, mine * rows, 0)
        yield total


def finish(steps):
    return list(steps)[-1].astype(jnp.float32)


def local(
    tokens,
    cotangent,
    segments,
    routes,
    capacity_slot,
    bucket_index,
    first_gain,
    query_projection_matrix,
    key_projection_matrix,
    value_projection_matrix,
    output_projection_matrix,
    position_bias,
    second_gain,
    router_weight,
    expert_in,
    expert_out,
):
    half_len, seq_count, model_width = tokens.shape
    tensor_count = lax.axis_size("tensor")
    seq_len = half_len * tensor_count
    owner_count = lax.axis_size("dp")
    local_inner = query_projection_matrix.shape[1]
    head_count = local_inner // HEAD_DIM
    expert_count = router_weight.shape[1]
    token_count = half_len * seq_count
    capacity = max(2, token_count * 5 // (4 * expert_count))
    pair_count = head_count // 2
    inputs = tokens.astype(jnp.float32)
    first_scale = rms_scale(inputs)
    gain_one = first_gain.astype(jnp.float32)
    normalized_rows = (inputs * first_scale * gain_one).astype(jnp.bfloat16)
    place = lax.axis_index("tensor")
    own_start = place * half_len
    other_start = half_len - own_start

    def swap(values):
        return lax.ppermute(values, "tensor", [(0, 1), (1, 0)])

    def gather_rows(values):
        whole = jnp.zeros((seq_len,) + values.shape[1:], values.dtype)
        whole = lax.dynamic_update_slice_in_dim(whole, swap(values), other_start, 0)
        return lax.dynamic_update_slice_in_dim(whole, values, own_start, 0)

    def scatter_rows(rows, multiply):
        theirs = multiply(lax.dynamic_slice_in_dim(rows, other_start, half_len, 0))
        received = swap(theirs.astype(jnp.bfloat16))
        own = multiply(lax.dynamic_slice_in_dim(rows, own_start, half_len, 0))
        return own + received.astype(jnp.float32)

    complete_rows = gather_rows(normalized_rows)
    flat_rows = complete_rows.reshape(seq_len, model_width)
    projected = [
        jnp.dot(flat_rows, matrix, preferred_element_type=jnp.float32).astype(jnp.bfloat16)
        for matrix in (query_projection_matrix, key_projection_matrix, value_projection_matrix)
    ]
    bucket_line = jnp.pad(bucket_index, (1, 0))
    bucket_back = jnp.pad(bucket_index[::-1], (1, 0))
    bucket_ids = jnp.arange(position_bias.shape[0], dtype=jnp.int32)[None, :]
    both_lines = jnp.dot(
        position_bias.T,
        (jnp.concatenate([bucket_line, bucket_back])[:, None] == bucket_ids).astype(jnp.bfloat16).T,
        preferred_element_type=jnp.float32,
    )
    forward_line = both_lines[:, : 2 * seq_len].reshape(pair_count, 2, 2 * seq_len)
    backward_line = both_lines[:, 2 * seq_len :].reshape(pair_count, 2, 2 * seq_len)
    lane_place = (jnp.arange(128, dtype=jnp.int32) % HEAD_DIM)[None, :]
    same_doc = segments == lane_place
    penalty = jnp.where(same_doc | (lane_place >= 8), 0.0, masked_score).astype(jnp.bfloat16)
    marks = jnp.where(
        lane_place < 8,
        same_doc.astype(jnp.float32),
        jnp.where(lane_place < 11, -1.0, 0.0),
    ).astype(jnp.bfloat16)
    block_rows = min(BLOCK_ROWS, seq_len)

    columns = pl.BlockSpec((seq_len, 128), lambda pair: (0, pair))

    whole_block = pl.BlockSpec((seq_len, 128), lambda pair: (0, 0))
    line_block = pl.BlockSpec((1, 2, 2 * seq_len), lambda pair: (pair, 0, 0))
    query_block = pl.BlockSpec((2, seq_len, 128), lambda pair: (pair, 0, 0))
    tile_shape = pltpu.VMEM((block_rows, 2 * seq_len), jnp.float32)
    head_outputs, query_rows = pl.pallas_call(
        attention_forward,
        grid=(pair_count,),
        in_specs=[columns, columns, columns, whole_block, whole_block, line_block],
        out_specs=[columns, query_block],
        out_shape=[
            jax.ShapeDtypeStruct((seq_len, local_inner), jnp.bfloat16),
            jax.ShapeDtypeStruct((head_count, seq_len, 128), jnp.bfloat16),
        ],
        scratch_shapes=[tile_shape],
        compiler_params=pltpu.CompilerParams(vmem_limit_bytes=48 << 20),
    )(*projected, penalty, marks, forward_line)
    head_outputs = head_outputs.reshape(seq_len, seq_count, local_inner)
    attention_result = scatter_rows(
        head_outputs,
        lambda rows: jnp.einsum(
            "awb,bk->awk", rows, output_projection_matrix, preferred_element_type=jnp.float32
        ),
    )
    mixed = inputs + attention_result
    second_scale = rms_scale(mixed)
    gain_two = second_gain.astype(jnp.float32)
    normed_two = (mixed * second_scale * gain_two).astype(jnp.bfloat16)
    normed_flat = normed_two.reshape(token_count, model_width)
    logits = jnp.dot(normed_flat, router_weight, preferred_element_type=jnp.float32)
    largest_logit = jnp.max(logits, axis=-1, keepdims=True)
    router_exp = jnp.exp(logits - largest_logit)
    router_probs = router_exp / jnp.sum(router_exp, axis=-1, keepdims=True)
    route_flat = routes.reshape(-1)
    slot_flat = capacity_slot.reshape(-1)
    kept_mask = slot_flat >= 0
    kept_float = kept_mask.astype(jnp.float32)
    route_hot = (route_flat[:, None] == jnp.arange(expert_count, dtype=jnp.int32)[None, :]).astype(
        jnp.float32
    )
    route_prob = jnp.sum(router_probs * route_hot, axis=-1)
    gate_value = route_prob * kept_float
    target = jnp.where(kept_mask, route_flat * capacity + slot_flat, expert_count * capacity)
    pack_hot = (
        jnp.arange(expert_count * capacity, dtype=jnp.int32)[:, None] == target[None, :]
    ).astype(jnp.bfloat16)

    first_matrix = expert_in[0]
    second_matrix = expert_out[0]
    grad_out = cotangent.astype(jnp.float32).reshape(token_count, model_width)
    grad_result = (gate_value[:, None] * grad_out).astype(jnp.bfloat16)
    packed = jnp.dot(
        pack_hot,
        jnp.concatenate([normed_flat, grad_result], axis=1),
        preferred_element_type=jnp.float32,
    ).astype(jnp.bfloat16)
    arrived = lax.all_to_all(
        packed.reshape(expert_count, capacity, 2 * model_width),
        "dp",
        split_axis=0,
        concat_axis=0,
        tiled=True,
    )
    arrived = arrived.reshape(-1, 2 * model_width)
    row_count = arrived.shape[0]
    all_rows = jnp.concatenate([arrived, swap(arrived)], axis=0)
    expert_rows = all_rows[:, :model_width]
    grad_rows_all = all_rows[:, model_width:]
    pre_act = jnp.dot(expert_rows, first_matrix, preferred_element_type=jnp.float32)
    hidden = smooth_gate(pre_act).astype(jnp.bfloat16)
    grad_hidden = jnp.dot(grad_rows_all, second_matrix.T, preferred_element_type=jnp.float32)
    gelu_value, gelu_pull = jax.vjp(smooth_gate, pre_act)
    grad_pre = gelu_pull(grad_hidden)[0].astype(jnp.bfloat16)

    def results(part):
        return jnp.concatenate(
            [
                jnp.dot(hidden[part], second_matrix, preferred_element_type=jnp.float32).astype(
                    jnp.bfloat16
                ),
                jnp.dot(grad_pre[part], first_matrix.T, preferred_element_type=jnp.float32).astype(
                    jnp.bfloat16
                ),
            ],
            axis=1,
        )

    received = swap(results(slice(row_count, 2 * row_count)))
    summed = results(slice(0, row_count)) + received
    returned = lax.all_to_all(
        summed.reshape(owner_count, capacity, 2 * model_width),
        "dp",
        split_axis=0,
        concat_axis=0,
        tiled=True,
    ).reshape(expert_count * capacity, 2 * model_width)
    grad_second = jnp.dot(hidden.T, grad_rows_all, preferred_element_type=jnp.float32)
    grad_first = jnp.dot(expert_rows.T, grad_pre, preferred_element_type=jnp.float32)
    unpacked = lax.dot_general(
        pack_hot, returned, (((0,), (0,)), ((), ())), preferred_element_type=jnp.float32
    )
    expert_tokens = unpacked[:, :model_width]
    mixed_flat = mixed.reshape(token_count, model_width)
    layer_out = (
        (mixed_flat + gate_value[:, None] * expert_tokens)
        .astype(jnp.bfloat16)
        .reshape(half_len, seq_count, model_width)
    )
    grad_gate = jnp.sum(grad_out * expert_tokens, axis=-1)
    grad_normed_two = unpacked[:, model_width:]
    grad_kept = grad_gate * kept_float
    grad_logits = (router_probs * (route_hot - route_prob[:, None]) * grad_kept[:, None]).astype(
        jnp.bfloat16
    )
    router_part = jnp.dot(normed_flat.T, grad_logits, preferred_element_type=jnp.float32)
    grad_normed_two = grad_normed_two + jnp.dot(
        grad_logits, router_weight.T, preferred_element_type=jnp.float32
    )
    scale_flat = second_scale.reshape(token_count, 1)
    second_part = jnp.sum(grad_normed_two * mixed_flat * scale_flat, axis=0)
    scaled_two = grad_normed_two * gain_two
    grad_mixed = (
        grad_out
        + scale_flat * scaled_two
        - mixed_flat
        * scale_flat
        * scale_flat
        * scale_flat
        * jnp.mean(mixed_flat * scaled_two, axis=-1, keepdims=True)
    )
    grad_attended = grad_mixed.astype(jnp.bfloat16).reshape(half_len, seq_count, model_width)
    gradient_attention_total = gather_rows(grad_attended)
    output_part = jnp.einsum(
        "bkn,bkx->nx", head_outputs, gradient_attention_total, preferred_element_type=jnp.float32
    )
    grad_heads = jnp.einsum(
        "zur,yr->zuy",
        gradient_attention_total,
        output_projection_matrix,
        preferred_element_type=jnp.float32,
    ).astype(jnp.bfloat16)
    grad_heads = grad_heads.reshape(seq_len, local_inner)
    grad_heads, output_part = lax.optimization_barrier((grad_heads, output_part))

    def pair_backward(pair, grad_heads):
        pair_columns = pl.BlockSpec((seq_len, 128), lambda step: (0, pair))
        return pl.pallas_call(
            attention_backward,
            grid=(1,),
            in_specs=[
                pl.BlockSpec((2, seq_len, 128), lambda step: (pair, 0, 0)),
                pair_columns,
                pair_columns,
                whole_block,
                pair_columns,
                pair_columns,
                pl.BlockSpec((1, 2, 2 * seq_len), lambda step: (pair, 0, 0)),
            ],
            out_specs=[
                pl.BlockSpec((seq_len, 384), lambda step: (0, 0)),
                line_block,
            ],
            out_shape=[
                jax.ShapeDtypeStruct((seq_len, 384), jnp.bfloat16),
                jax.ShapeDtypeStruct((1, 2, 2 * seq_len), jnp.float32),
            ],
            scratch_shapes=[
                tile_shape,
                tile_shape,
                pltpu.VMEM((seq_len, 128), jnp.float32),
            ],
            compiler_params=pltpu.CompilerParams(vmem_limit_bytes=48 << 20),
            cost_estimate=pl.CostEstimate(
                flops=20 * 128 * seq_len * seq_len,
                bytes_accessed=20 * 128 * seq_len,
                transcendentals=2 * seq_len * seq_len,
            ),
        )(
            query_rows,
            projected[1],
            projected[2],
            marks,
            head_outputs.reshape(seq_len, local_inner),
            grad_heads,
            backward_line,
        )

    output_steps = halving_steps(output_part, 1)
    running = [output_steps]
    pair_grads, line_grads = [], []
    for pair in range(pair_count):
        pair_grad, pair_line = pair_backward(pair, grad_heads)
        pair_grads.append(pair_grad)
        line_grads.append(pair_line)
        if pair < pair_count - 1:
            under_way = [next(steps) for steps in running]
            grad_heads, pair_grad, *_ = lax.optimization_barrier(
                (grad_heads, pair_grad, *under_way)
            )
        pair_part = jnp.dot(flat_rows.T, pair_grad, preferred_element_type=jnp.float32)
        if pair < pair_count - 1:
            grad_heads, pair_part = lax.optimization_barrier((grad_heads, pair_part))
        running.append(halving_steps(pair_part, pair))
    line_grad = jnp.concatenate(line_grads, axis=0)
    bias_part_total = jnp.dot(
        (bucket_back[:, None] == bucket_ids).astype(jnp.float32).T,
        line_grad.reshape(head_count, 2 * seq_len).T,
        precision=exact_precision,
    )
    gradient_rows = jnp.concatenate(pair_grads, axis=1)[:, None, :]
    pair_matrices = jnp.concatenate(
        [
            matrix[:, 128 * pair : 128 * (pair + 1)]
            for pair in range(pair_count)
            for matrix in (
                query_projection_matrix,
                key_projection_matrix,
                value_projection_matrix,
            )
        ],
        axis=1,
    )
    grad_normed = scatter_rows(
        gradient_rows,
        lambda rows: jnp.einsum(
            "ybq,gq->ybg", rows, pair_matrices, preferred_element_type=jnp.float32
        ),
    )
    first_part = jnp.sum(grad_normed * inputs * first_scale, axis=(0, 1))
    scaled_one = grad_normed * gain_one
    grad_mixed_grid = grad_mixed.reshape(half_len, seq_count, model_width)
    tokens_grad = (
        grad_mixed_grid
        + first_scale * scaled_one
        - inputs
        * first_scale
        * first_scale
        * first_scale
        * jnp.mean(inputs * scaled_one, axis=-1, keepdims=True)
    )
    early_part = jnp.concatenate([router_part.reshape(-1), second_part])
    early_grad = exchange_sum(early_part + swap(early_part))
    first_part = first_part + swap(first_part)
    late_grad = exchange_sum(jnp.concatenate([first_part, bias_part_total.reshape(-1)]))
    first_gain_grad = late_grad[:model_width]
    position_bias_grad = late_grad[model_width:].reshape(bias_part_total.shape)
    router_grad = early_grad[: router_part.size].reshape(router_part.shape)
    second_gain_grad = early_grad[router_part.size :]
    output_grad, *pair_sums = [finish(steps) for steps in running]
    query_grad, key_grad, value_grad = [
        jnp.concatenate([part[:, 128 * group : 128 * (group + 1)] for part in pair_sums], axis=1)
        for group in range(3)
    ]
    return (
        layer_out,
        tokens_grad.astype(jnp.bfloat16),
        first_gain_grad,
        query_grad,
        key_grad,
        value_grad,
        output_grad,
        position_bias_grad,
        second_gain_grad,
        router_grad,
        grad_first[None],
        grad_second[None],
    )


def solution(mesh):
    return jax.shard_map(
        local,
        mesh=mesh,
        in_specs=(
            P("tensor", "dp", None),
            P("tensor", "dp", None),
            P(None, "dp"),
            P("tensor", "dp"),
            P("tensor", "dp"),
            P(),
            P(),
            P(None, "tensor"),
            P(None, "tensor"),
            P(None, "tensor"),
            P("tensor", None),
            P(None, "tensor"),
            P(),
            P(),
            P("dp", None, "tensor"),
            P("dp", "tensor", None),
        ),
        out_specs=(
            P("tensor", "dp", None),
            P("tensor", "dp", None),
            P(),
            P(None, "tensor"),
            P(None, "tensor"),
            P(None, "tensor"),
            P("tensor", None),
            P(None, "tensor"),
            P(),
            P(),
            P("dp", None, "tensor"),
            P("dp", "tensor", None),
        ),
        check_vma=False,
    )
```
